32 devices in a mesh: dom: 2 (over x), term: 16 (over z, y, core).
Axes of the slice: x: 2, y: 2, z: 4, core: 2. Of those that a mesh axis runs over, the one named last changes fastest.
Arguments:
- tile_values: bfloat16 [3072, 128, 128], P(('dom', 'term')), parts along dimension 0, may hold values from -6 to 6
- tile_doc: int32 [3072], P(('dom', 'term')), parts along dimension 0, may hold values from 0 to 31, as said below
- tile_col: int32 [3072], P(('dom', 'term')), parts along dimension 0, may hold values from 0 to 31
- tile_count: int32 [32], P('dom'), parts along dimension 0, may hold values from 1 to 96, as said below
- panel: bfloat16 [65536, 256], P('term'), may hold values from -6 to 6
Outputs:
- panel_next: float32 [131072, 256], P(('dom', 'term')), parts along dimension 0
The draws below stay inside these ranges and needn't reach their ends.
There are 2 independent parts, one for each index of `dom`. The reference program is written for one: setup_inputs(seed, part) draws one part's arguments, and reference() takes and returns one part's arrays. A program takes and returns all parts, laid end to end along the dimension named above; an argument that names none is the same for every part. Nothing has to cross between parts.
Inputs may be any that keep to these rules, and one draw needn't show every extreme that they name: Within one device's 96 slots the pairs (tile_doc, tile_col) are all different. Slots of device d at or above tile_count[d] are not part of the matrix; terms are in order of falling frequency, so tile_count[d] lies between 96 - 77 * d // 15 - 12 and 96 - 77 * d // 15, and tile_count[0] is 96.
All inputs are finite; a program needn't handle non-finite values.
Results may differ from the reference program's by a relative error of at most 0.0095.
Values may be sent and summed in bfloat16 or wider, within the bound.
A program may use at most 64 MiB of HBM per device.

```python
import jax
import jax.numpy as jnp
from jax import lax

TILE = 128
RANK = 256
TERM_BLKS = 32
DOC_BLKS = 32
CAP = 96
TERMS = 65536
N_TERM = 16


def tile_layout(key):
    device_keys = jax.random.split(key, N_TERM)
    places = jax.vmap(lambda one_key: jax.random.permutation(one_key, DOC_BLKS * TERM_BLKS))(device_keys)
    return places[:, :CAP].reshape(-1).astype(jnp.int32)


def draw_tile_doc(key, part):
    return tile_layout(key) // TERM_BLKS


def draw_tile_col(key, part):
    return tile_layout(key) % TERM_BLKS


def draw_tile_count(key, part):
    key = jax.random.fold_in(key, 7)
    index = jnp.arange(N_TERM, dtype=jnp.int32)
    trend = CAP - (CAP - CAP // 5) * index // (N_TERM - 1)
    jitter = jax.random.randint(key, (N_TERM,), 0, CAP // 8 + 1)
    jitter = jnp.where(index == 0, 0, jitter)
    return jnp.maximum(trend - jitter, 1).astype(jnp.int32)


def shard_levels(stream_key, extent, cuts, least, largest):
    def one(dim, shards_of):
        steps = jax.random.uniform(jax.random.fold_in(jax.random.fold_in(stream_key, 6), dim), (shards_of,), jnp.float32, least / len(cuts), largest / len(cuts))
        return jnp.repeat(jnp.exp(steps), extent[dim] // shards_of).reshape((-1,) + (1,) * (len(extent) - dim - 1))

    factor_of = one(*cuts[0])
    for cut in cuts[1:]:
        factor_of = factor_of * one(*cut)
    return factor_of


def gaussian(stream_key, shape, width, most, shards=(), kind=jnp.bfloat16):
    array = jax.random.normal(stream_key, shape, jnp.float32) * width
    if len(shards) > 0:
        array = shard_levels(stream_key, shape, shards, -0.22, 0.18) * array
    return jnp.clip(array, min=-most, max=most).astype(kind)


def setup_inputs(seed: int = 0, part: int = 0) -> dict:
    arg_keys = jax.random.split(jax.random.key(seed), 6)
    own_keys = jax.random.split(jax.random.fold_in(arg_keys[5], part), 6)
    return {
        "tile_values": gaussian(own_keys[0], (N_TERM * CAP, TILE, TILE), 1.0, 6.0, ((0, 16),)),
        "tile_doc": draw_tile_doc(jax.random.fold_in(jax.random.fold_in(arg_keys[5], part), 71), part),
        "tile_col": draw_tile_col(jax.random.fold_in(jax.random.fold_in(arg_keys[5], part), 71), part),
        "tile_count": draw_tile_count(jax.random.fold_in(jax.random.fold_in(arg_keys[5], part), 71), part),
        "panel": gaussian(arg_keys[4], (TERMS, RANK), 1.0, 6.0, ((0, 16),)),
    }


shift_ratio = 0.001

def factor(gram_matrix):
    rank_width = gram_matrix.shape[0]
    shifted = gram_matrix + shift_ratio * jnp.trace(gram_matrix) / rank_width * jnp.eye(rank_width, dtype=jnp.float32)
    return jnp.linalg.cholesky(shifted)

def whiten(chol_lower, row_block):
    return jax.scipy.linalg.solve_triangular(chol_lower, row_block.T, lower=True).T

def reference(tile_values, tile_doc, tile_col, tile_count, panel):
    tiles_all = tile_values.reshape(N_TERM, CAP, TILE, TILE)
    docs_all = tile_doc.reshape(N_TERM, CAP)
    cols_all = tile_col.reshape(N_TERM, CAP)
    q_all = panel.reshape(N_TERM, TERM_BLKS, TILE, RANK)
    slot_ids = jnp.arange(CAP, dtype=jnp.int32)
    doc_ids = jnp.arange(DOC_BLKS, dtype=jnp.int32)
    col_ids = jnp.arange(TERM_BLKS, dtype=jnp.int32)

    def add_device(summed, device_item):
        tiles_dev, docs_dev, cols_dev, count_dev, q_dev = device_item
        live_mask = (slot_ids < count_dev).astype(jnp.float32)
        picked = q_dev[cols_dev].astype(jnp.float32)
        products = jnp.einsum('sij,sjr->sir', tiles_dev.astype(jnp.float32), picked)
        one_hot = (docs_dev[:, None] == doc_ids[None, :]).astype(jnp.float32) * live_mask[:, None]
        return (summed + jnp.einsum('sd,sir->dir', one_hot, products), None)
    start_sum = jnp.zeros((DOC_BLKS, TILE, RANK), jnp.float32)
    doc_sums, _ = lax.scan(add_device, start_sum, (tiles_all, docs_all, cols_all, tile_count, q_all))
    doc_rows = doc_sums.reshape(DOC_BLKS * TILE, RANK)
    gram_matrix = jnp.dot(doc_rows.T, doc_rows, precision=lax.Precision.HIGHEST)
    ortho_rows = whiten(factor(gram_matrix), doc_rows).astype(jnp.bfloat16)
    ortho_blocks = ortho_rows.reshape(DOC_BLKS, TILE, RANK)

    def project(device_item):
        tiles_dev, docs_dev, cols_dev, count_dev = device_item
        live_mask = (slot_ids < count_dev).astype(jnp.float32)
        picked = ortho_blocks[docs_dev].astype(jnp.float32)
        products = jnp.einsum('sij,sir->sjr', tiles_dev.astype(jnp.float32), picked)
        one_hot = (cols_dev[:, None] == col_ids[None, :]).astype(jnp.float32) * live_mask[:, None]
        return jnp.einsum('sc,sjr->cjr', one_hot, products)
    blocks_out = lax.map(project, (tiles_all, docs_all, cols_all, tile_count))
    return blocks_out.reshape(N_TERM * TERM_BLKS * TILE, RANK)
```

```python
import functools

import jax
import jax.numpy as jnp
from jax import lax
from jax.experimental import pallas as pl
from jax.experimental.pallas import tpu as pltpu
from jax.sharding import PartitionSpec as P

DOC_BLKS = 32
GROUP = 4
MIB = 1024 * 1024

shift_ratio = 0.001


def each_slot(count, body):
    whole = count // GROUP

    def group(index, carry):
        body([index * GROUP + k for k in range(GROUP)])
        return carry

    def single(index, carry):
        body([index])
        return carry

    lax.fori_loop(0, whole, group, 0)
    lax.fori_loop(whole * GROUP, count, single, 0)


def forward_kernel(count_ref, doc_ref, col_ref, tiles_ref, panel_ref, rows_ref, total):
    tile = tiles_ref.shape[1]
    count = count_ref[lax.axis_index("term")]
    total[...] = jnp.zeros_like(total)

    def body(slots):
        products = []
        for slot in slots:
            start = pl.multiple_of(col_ref[slot] * tile, tile)
            products.append(
                jnp.dot(
                    tiles_ref[slot],
                    panel_ref[pl.ds(start, tile), :],
                    preferred_element_type=jnp.float32,
                )
            )
        for slot, product in zip(slots, products):
            start = pl.multiple_of(doc_ref[slot] * tile, tile)
            total[pl.ds(start, tile), :] += product

    each_slot(count, body)
    rows_ref[...] = total[...].astype(rows_ref.dtype)


def exchange_kernel(n, chunks, orders, x_ref, y_ref, *scratch):
    stages = len(orders[0])
    recv_bufs = scratch[:stages]
    send_bufs = scratch[stages : 2 * stages - 1]
    keep_bufs = scratch[2 * stages - 1 : 3 * stages - 2]
    send_sems, recv_sems = scratch[3 * stages - 2 :]
    me = lax.axis_index("term")
    rows = x_ref.shape[0] // chunks

    def bit_of(bit):
        return (me // (1 << bit)) % 2

    def partner(bit):
        return me + (1 << bit) - 2 * (1 << bit) * bit_of(bit)

    barrier = pltpu.get_barrier_semaphore()
    for bit in range(stages):
        pl.semaphore_signal(
            barrier, inc=1, device_id={"term": partner(bit)}, device_id_type=pl.DeviceIdType.MESH
        )
    pl.semaphore_wait(barrier, stages)

    started = []

    def send(phase, stage, chunk, bit, src, dst):
        copy = pltpu.make_async_remote_copy(
            src_ref=src,
            dst_ref=dst,
            send_sem=send_sems.at[phase, stage, chunk],
            recv_sem=recv_sems.at[phase, stage, chunk],
            device_id={"term": partner(bit)},
            device_id_type=pl.DeviceIdType.MESH,
        )
        copy.start()
        started.append(copy)
        return copy

    offsets = [[None] * (stages + 1) for _ in range(chunks)]
    reduce_copies = [[None] * stages for _ in range(chunks)]
    for chunk in range(chunks):
        offset = chunk * rows
        offsets[chunk][0] = offset
        for stage, bit in enumerate(orders[chunk]):
            half = rows >> (stage + 1)
            offset = offset + bit_of(bit) * half
            offsets[chunk][stage + 1] = offset
        half = rows // 2
        bit = orders[chunk][0]
        away = pl.multiple_of(chunk * rows + (1 - bit_of(bit)) * half, 16)
        reduce_copies[chunk][0] = send(
            0, 0, chunk, bit, x_ref.at[pl.ds(away, half)], recv_bufs[0].at[chunk]
        )

    def add_into(count, dst, dst_at, left, left_at, right, right_at):
        step = min(count, 64)

        def piece(index, carry):
            at = index * step

            def where(base):
                return pl.ds(pl.multiple_of(base + at, 16), step)

            value = left[where(left_at), :].astype(jnp.float32) + right[where(right_at), :].astype(
                jnp.float32
            )
            dst[where(dst_at), :] = value.astype(dst.dtype)
            return carry

        lax.fori_loop(0, count // step, piece, 0)

    gather_copies = [[None] * stages for _ in range(chunks)]

    def start_gather(chunk, stage):
        size = rows >> (stage + 1)
        at = pl.multiple_of(offsets[chunk][stage + 1], 16)
        block = y_ref.at[pl.ds(at, size)]
        gather_copies[chunk][stage] = send(1, stage, chunk, orders[chunk][stage], block, block)

    for stage in range(stages):
        size = rows >> (stage + 1)
        for chunk in range(chunks):
            reduce_copies[chunk][stage].wait_recv()
            got = recv_bufs[stage].at[chunk]
            if stage == 0:
                held, held_at = x_ref, offsets[chunk][1]
            else:
                held, held_at = keep_bufs[stage - 1].at[chunk], 0
            if stage == stages - 1:
                add_into(size, y_ref, offsets[chunk][stages], held, held_at, got, 0)
                start_gather(chunk, stage)
            else:
                bit = orders[chunk][stage + 1]
                half = size // 2
                mine, other = bit_of(bit) * half, (1 - bit_of(bit)) * half
                out = send_bufs[stage].at[chunk]
                add_into(half, out, 0, held, held_at + other, got, other)
                reduce_copies[chunk][stage + 1] = send(
                    0, stage + 1, chunk, bit, out, recv_bufs[stage + 1].at[chunk]
                )
                add_into(half, keep_bufs[stage].at[chunk], 0, held, held_at + mine, got, mine)

    for stage in reversed(range(stages)):
        for chunk in range(chunks):
            gather_copies[chunk][stage].wait_recv()
            if stage > 0:
                start_gather(chunk, stage - 1)
    for copy in started:
        copy.wait_send()


def dot32(a, b, dims):
    return lax.dot_general(
        a, b, (dims, ((), ())), precision=lax.Precision.HIGHEST, preferred_element_type=jnp.float32
    )


def backward_kernel(
    count_ref, doc_ref, col_ref, tiles_ref, rows_ref, out_ref, ortho, inverse, matrix
):
    tile = tiles_ref.shape[1]
    rank = rows_ref.shape[1]
    count = count_ref[lax.axis_index("term")]
    depth = 512
    matrix[...] = jnp.zeros_like(matrix)

    def gram_step(index, carry):
        block = rows_ref[pl.ds(pl.multiple_of(index * depth, depth), depth), :]
        matrix[...] += lax.dot_general(
            block, block, (((0,), (0,)), ((), ())), preferred_element_type=jnp.float32
        )
        return carry

    lax.fori_loop(0, rows_ref.shape[0] // depth, gram_step, 0)
    row_ids = lax.broadcasted_iota(jnp.int32, (rank, rank), 0)
    lane_ids = lax.broadcasted_iota(jnp.int32, (rank, rank), 1)
    eye = (row_ids == lane_ids).astype(jnp.float32)
    gram = matrix[...]
    shift = shift_ratio * jnp.sum(gram * eye) / rank
    gram = gram + shift * eye
    scale_row = lax.rsqrt(jnp.sum(gram * eye, axis=0, keepdims=True))
    scale_col = lax.rsqrt(jnp.sum(gram * eye, axis=1, keepdims=True))
    gram = gram * scale_row * scale_col
    matrix[...] = gram
    inverse[...] = eye
    half_lower = jnp.where(row_ids > lane_ids, 1.0, jnp.where(row_ids == lane_ids, 0.5, 0.0))

    def unsolved(state):
        index, error = state
        return jnp.logical_and(index < 12, jnp.logical_not(error < 1e-6))

    def newton(state):
        index, _ = state
        now = inverse[...]
        left = dot32(now, matrix[...], ((1,), (0,)))
        gap = dot32(left, now, ((1,), (1,))) - eye
        inverse[...] = now - dot32(gap * half_lower, now, ((1,), (0,)))
        return index + 1, jnp.sum(gap * gap)

    _, error = lax.while_loop(unsolved, newton, (0, jnp.float32(1e30)))

    @pl.when(jnp.logical_not(error < 1e-6))
    def _():
        inverse[...] = eye
        lanes = lax.broadcasted_iota(jnp.int32, (1, rank), 1)

        def column(index, carry):
            pivot_row = matrix[pl.ds(index, 1), :]
            pivot = jnp.sum(jnp.where(lanes == index, pivot_row, 0.0), axis=1, keepdims=True)
            root = lax.rsqrt(pivot)
            factors = jnp.sum(
                jnp.where(lane_ids == index, matrix[...], 0.0), axis=1, keepdims=True
            )
            factors = jnp.where(row_ids[:, :1] > index, factors * root, 0.0)
            solved = inverse[pl.ds(index, 1), :] * root
            matrix[...] -= factors * (pivot_row * root)
            inverse[...] -= factors * solved
            inverse[pl.ds(index, 1), :] = solved
            return carry

        lax.fori_loop(0, rank, column, 0)

    whitener = (inverse[...] * scale_row).astype(jnp.bfloat16)

    def whiten_step(index, carry):
        where = pl.ds(pl.multiple_of(index * depth, depth), depth)
        ortho[where, :] = lax.dot_general(
            rows_ref[where, :],
            whitener,
            (((1,), (1,)), ((), ())),
            preferred_element_type=jnp.float32,
        ).astype(jnp.bfloat16)
        return carry

    lax.fori_loop(0, rows_ref.shape[0] // depth, whiten_step, 0)
    out_ref[...] = jnp.zeros_like(out_ref)

    def body(slots):
        products = []
        for slot in slots:
            start = pl.multiple_of(doc_ref[slot] * tile, tile)
            products.append(
                lax.dot_general(
                    tiles_ref[slot],
                    ortho[pl.ds(start, tile), :],
                    (((0,), (0,)), ((), ())),
                    preferred_element_type=jnp.float32,
                )
            )
        for slot, product in zip(slots, products):
            start = pl.multiple_of(col_ref[slot] * tile, tile)
            out_ref[pl.ds(start, tile), :] += product

    each_slot(count, body)


def exchange(rows, n):
    bits = n.bit_length() - 1
    height, rank = rows.shape
    chunks = max(1, min(4, height // (16 * n)))
    plain = list(range(bits))
    swapped = [0, 2, 1] + plain[3:] if bits > 2 else plain
    orders = [swapped if chunk == chunks - 1 and chunks > 1 else plain for chunk in range(chunks)]
    size = height // chunks
    scratch = [pltpu.VMEM((chunks, size >> (k + 1), rank), jnp.bfloat16) for k in range(bits)]
    scratch += [pltpu.VMEM((chunks, size >> (k + 2), rank), jnp.bfloat16) for k in range(bits - 1)]
    scratch += [pltpu.VMEM((chunks, size >> (k + 2), rank), jnp.float32) for k in range(bits - 1)]
    scratch += [pltpu.SemaphoreType.DMA((2, bits, chunks))] * 2
    return pl.pallas_call(
        functools.partial(exchange_kernel, n, chunks, orders),
        out_shape=jax.ShapeDtypeStruct(rows.shape, jnp.bfloat16),
        in_specs=[pl.BlockSpec(memory_space=pltpu.VMEM)],
        out_specs=pl.BlockSpec(memory_space=pltpu.VMEM),
        scratch_shapes=scratch,
        compiler_params=pltpu.CompilerParams(
            collective_id=0, has_side_effects=True, vmem_limit_bytes=40 * MIB
        ),
        name="exchange",
    )(rows)


def local(n, tile_values, tile_doc, tile_col, tile_count, panel):
    tile = tile_values.shape[1]
    rank = panel.shape[1]
    height = DOC_BLKS * tile
    smem = pl.BlockSpec(memory_space=pltpu.SMEM)
    vmem = pl.BlockSpec(memory_space=pltpu.VMEM)
    params = pltpu.CompilerParams(vmem_limit_bytes=40 * MIB)
    rows = pl.pallas_call(
        forward_kernel,
        out_shape=jax.ShapeDtypeStruct((height, rank), jnp.bfloat16),
        in_specs=[smem, smem, smem, vmem, vmem],
        out_specs=vmem,
        scratch_shapes=[pltpu.VMEM((height, rank), jnp.float32)],
        compiler_params=params,
        name="forward",
    )(tile_count, tile_doc, tile_col, tile_values, panel)
    rows = exchange(rows, n)
    return pl.pallas_call(
        backward_kernel,
        out_shape=jax.ShapeDtypeStruct(panel.shape, jnp.float32),
        in_specs=[smem, smem, smem, vmem, vmem],
        out_specs=vmem,
        scratch_shapes=[
            pltpu.VMEM((height, rank), jnp.bfloat16),
            pltpu.VMEM((rank, rank), jnp.float32),
            pltpu.VMEM((rank, rank), jnp.float32),
        ],
        compiler_params=params,
        name="backward",
    )(tile_count, tile_doc, tile_col, tile_values, rows)


def solution(mesh):
    return jax.shard_map(
        functools.partial(local, mesh.shape["term"]),
        mesh=mesh,
        in_specs=(
            P(("dom", "term"), None, None),
            P(("dom", "term")),
            P(("dom", "term")),
            P("dom"),
            P("term", None),
        ),
        out_specs=P(("dom", "term"), None),
        check_vma=False,
    )
```

```python
import functools

import jax
import jax.numpy as jnp
from jax import lax
from jax.experimental import pallas as pl
from jax.experimental.pallas import tpu as pltpu
from jax.sharding import PartitionSpec as P

DOC_BLKS = 32
GROUP = 8
MIB = 1024 * 1024

shift_ratio = 0.001


def each_slot(count, body):
    whole = count // GROUP

    def group(index, carry):
        body([index * GROUP + k for k in range(GROUP)])
        return carry

    def single(index, carry):
        body([index])
        return carry

    lax.fori_loop(0, whole, group, 0)
    lax.fori_loop(whole * GROUP, count, single, 0)


def start_copies(sources, targets, sems):
    copies = [
        pltpu.make_async_copy(source, target, sems.at[index])
        for index, (source, target) in enumerate(zip(sources, targets))
    ]
    for copy in copies:
        copy.start()
    return copies


def forward_kernel(
    count_hbm, doc_hbm, col_hbm, tiles_hbm, panel_hbm, rows_ref,
    count_ref, doc_ref, col_ref, tiles_ref, panel_ref, total, sems,
):
    tile = tiles_ref.shape[1]
    copies = start_copies(
        (count_hbm, doc_hbm, col_hbm, panel_hbm, tiles_hbm),
        (count_ref, doc_ref, col_ref, panel_ref, tiles_ref),
        sems,
    )
    total[...] = jnp.zeros_like(total)
    for copy in copies:
        copy.wait()
    count = count_ref[lax.axis_index("term")]

    def body(slots):
        products = []
        for slot in slots:
            start = pl.multiple_of(col_ref[slot] * tile, tile)
            products.append(
                jnp.dot(
                    tiles_ref[slot],
                    panel_ref[pl.ds(start, tile), :],
                    preferred_element_type=jnp.float32,
                )
            )
        for slot, product in zip(slots, products):
            start = pl.multiple_of(doc_ref[slot] * tile, tile)
            total[pl.ds(start, tile), :] += product

    each_slot(count, body)
    rows_ref[...] = total[...].astype(rows_ref.dtype)


def exchange_kernel(chunks, orders, x_ref, y_ref, gram_ref, *scratch):
    stages = len(orders[0])
    recv_bufs = scratch[:stages]
    send_bufs = scratch[stages : 2 * stages - 1]
    keep_bufs = scratch[2 * stages - 1 : 3 * stages - 2]
    send_sems, recv_sems = scratch[3 * stages - 2 :]
    me = lax.axis_index("term")
    rows = x_ref.shape[0] // chunks

    def width(bit):
        if isinstance(bit, tuple):
            return (1 << bit[0]) + ((1 << bit[1]) - (1 << bit[0])) * (me % 2)
        return 1 << bit

    def bit_of(bit):
        return (me // width(bit)) % 2

    def partner(bit):
        return me + width(bit) - 2 * width(bit) * bit_of(bit)

    barrier = pltpu.get_barrier_semaphore()
    bits = list(dict.fromkeys(bit for order in orders for bit in order))
    for bit in bits:
        pl.semaphore_signal(
            barrier, inc=1, device_id={"term": partner(bit)}, device_id_type=pl.DeviceIdType.MESH
        )
    pl.semaphore_wait(barrier, len(bits))

    started = []

    def send(phase, stage, chunk, bit, src, dst):
        copy = pltpu.make_async_remote_copy(
            src_ref=src,
            dst_ref=dst,
            send_sem=send_sems.at[phase, stage, chunk],
            recv_sem=recv_sems.at[phase, stage, chunk],
            device_id={"term": partner(bit)},
            device_id_type=pl.DeviceIdType.MESH,
        )
        copy.start()
        started.append(copy)
        return copy

    offsets = [[None] * (stages + 1) for _ in range(chunks)]
    reduce_copies = [[None] * stages for _ in range(chunks)]
    for chunk in range(chunks):
        offset = chunk * rows
        offsets[chunk][0] = offset
        for stage, bit in enumerate(orders[chunk]):
            half = rows >> (stage + 1)
            offset = offset + bit_of(bit) * half
            offsets[chunk][stage + 1] = offset
        half = rows // 2
        bit = orders[chunk][0]
        away = pl.multiple_of(chunk * rows + (1 - bit_of(bit)) * half, 16)
        reduce_copies[chunk][0] = send(
            0, 0, chunk, bit, x_ref.at[pl.ds(away, half)], recv_bufs[0].at[chunk]
        )

    def add_into(count, dst, dst_at, left, left_at, right, right_at):
        step = min(count, 64)

        def piece(index, carry):
            at = index * step

            def where(base):
                return pl.ds(pl.multiple_of(base + at, 16), step)

            value = left[where(left_at), :].astype(jnp.float32) + right[where(right_at), :].astype(
                jnp.float32
            )
            dst[where(dst_at), :] = value.astype(dst.dtype)
            return carry

        lax.fori_loop(0, count // step, piece, 0)

    gather_copies = [[None] * stages for _ in range(chunks)]

    def start_gather(chunk, stage):
        size = rows >> (stage + 1)
        at = pl.multiple_of(offsets[chunk][stage + 1], 16)
        block = y_ref.at[pl.ds(at, size)]
        gather_copies[chunk][stage] = send(1, stage, chunk, orders[chunk][stage], block, block)

    def reduce_step(stage, chunk):
        size = rows >> (stage + 1)
        reduce_copies[chunk][stage].wait_recv()
        got = recv_bufs[stage].at[chunk]
        if stage == 0:
            held, held_at = x_ref, offsets[chunk][1]
        else:
            held, held_at = keep_bufs[stage - 1].at[chunk], 0
        if stage == stages - 1:
            add_into(size, y_ref, offsets[chunk][stages], held, held_at, got, 0)
            start_gather(chunk, stage)
        else:
            bit = orders[chunk][stage + 1]
            half = size // 2
            mine, other = bit_of(bit) * half, (1 - bit_of(bit)) * half
            out = send_bufs[stage].at[chunk]
            add_into(half, out, 0, held, held_at + other, got, other)
            reduce_copies[chunk][stage + 1] = send(
                0, stage + 1, chunk, bit, out, recv_bufs[stage + 1].at[chunk]
            )
            add_into(half, keep_bufs[stage].at[chunk], 0, held, held_at + mine, got, mine)

    gram_ref[...] = jnp.zeros_like(gram_ref)

    def gather_step(stage, chunk):
        gather_copies[chunk][stage].wait_recv()
        if stage > 0:
            start_gather(chunk, stage - 1)
        else:
            block = y_ref[chunk * rows : (chunk + 1) * rows, :]
            gram_ref[...] += lax.dot_general(
                block, block, (((0,), (0,)), ((), ())), preferred_element_type=jnp.float32
            )

    for diagonal in range(2 * stages + chunks - 1):
        for chunk in range(chunks):
            step = diagonal - chunk
            if 0 <= step < stages:
                reduce_step(step, chunk)
            elif stages <= step < 2 * stages:
                gather_step(2 * stages - 1 - step, chunk)
    for copy in started:
        copy.wait_send()


def dot16(a, b, dims):
    return lax.dot_general(
        a.astype(jnp.bfloat16),
        b.astype(jnp.bfloat16),
        (dims, ((), ())),
        preferred_element_type=jnp.float32,
    )


def dot32(a, b, dims):
    return lax.dot_general(
        a, b, (dims, ((), ())), precision=lax.Precision.HIGHEST, preferred_element_type=jnp.float32
    )


def backward_kernel(
    count_hbm, doc_hbm, col_hbm, tiles_hbm, rows_ref, gram_ref, out_ref,
    count_ref, doc_ref, col_ref, tiles_ref, ortho, inverse, matrix, sems,
):
    tile = tiles_ref.shape[1]
    rank = rows_ref.shape[1]
    depth = 512
    copies = start_copies(
        (count_hbm, doc_hbm, col_hbm, tiles_hbm), (count_ref, doc_ref, col_ref, tiles_ref), sems
    )
    out_ref[...] = jnp.zeros_like(out_ref)
    row_ids = lax.broadcasted_iota(jnp.int32, (rank, rank), 0)
    lane_ids = lax.broadcasted_iota(jnp.int32, (rank, rank), 1)
    eye = (row_ids == lane_ids).astype(jnp.float32)
    gram = gram_ref[...]
    shift = shift_ratio * jnp.sum(gram * eye) / rank
    gram = gram + shift * eye
    scale_row = lax.rsqrt(jnp.sum(gram * eye, axis=0, keepdims=True))
    scale_col = lax.rsqrt(jnp.sum(gram * eye, axis=1, keepdims=True))
    gram = gram * scale_row * scale_col
    matrix[...] = gram
    inverse[...] = eye
    half_lower = jnp.where(row_ids > lane_ids, 1.0, jnp.where(row_ids == lane_ids, 0.5, 0.0))

    def newton(most, goal, dot):
        def unsolved(state):
            index, error = state
            return jnp.logical_and(index < most, jnp.logical_not(error < goal))

        def step(state):
            index, _ = state
            now = inverse[...]
            left = dot(now, matrix[...], ((1,), (0,)))
            gap = dot(left, now, ((1,), (1,))) - eye
            inverse[...] = now - dot(gap * half_lower, now, ((1,), (0,)))
            return index + 1, jnp.sum(gap * gap)

        _, error = lax.while_loop(unsolved, step, (0, jnp.float32(1e30)))
        return error

    newton(6, 0.1, dot16)
    error = newton(12, 1e-4, dot32)

    @pl.when(jnp.logical_not(error < 1e-4))
    def _():
        inverse[...] = eye
        lanes = lax.broadcasted_iota(jnp.int32, (1, rank), 1)

        def column(index, carry):
            pivot_row = matrix[pl.ds(index, 1), :]
            pivot = jnp.sum(jnp.where(lanes == index, pivot_row, 0.0), axis=1, keepdims=True)
            root = lax.rsqrt(pivot)
            factors = jnp.sum(
                jnp.where(lane_ids == index, matrix[...], 0.0), axis=1, keepdims=True
            )
            factors = jnp.where(row_ids[:, :1] > index, factors * root, 0.0)
            solved = inverse[pl.ds(index, 1), :] * root
            matrix[...] -= factors * (pivot_row * root)
            inverse[...] -= factors * solved
            inverse[pl.ds(index, 1), :] = solved
            return carry

        lax.fori_loop(0, rank, column, 0)

    whitener = (inverse[...] * scale_row).astype(jnp.bfloat16)

    def whiten_step(index, carry):
        where = pl.ds(pl.multiple_of(index * depth, depth), depth)
        ortho[where, :] = lax.dot_general(
            rows_ref[where, :],
            whitener,
            (((1,), (1,)), ((), ())),
            preferred_element_type=jnp.float32,
        ).astype(jnp.bfloat16)
        return carry

    lax.fori_loop(0, rows_ref.shape[0] // depth, whiten_step, 0)
    for copy in copies:
        copy.wait()
    count = count_ref[lax.axis_index("term")]

    def body(slots):
        products = []
        for slot in slots:
            start = pl.multiple_of(doc_ref[slot] * tile, tile)
            products.append(
                lax.dot_general(
                    tiles_ref[slot],
                    ortho[pl.ds(start, tile), :],
                    (((0,), (0,)), ((), ())),
                    preferred_element_type=jnp.float32,
                )
            )
        for slot, product in zip(slots, products):
            start = pl.multiple_of(col_ref[slot] * tile, tile)
            out_ref[pl.ds(start, tile), :] += product

    each_slot(count, body)


def orders_of(n, height):
    bits = n.bit_length() - 1
    order = [0, (2, 1), (1, 2)] + list(range(3, bits)) if bits > 2 else list(range(bits))
    return [order] * max(1, min(4, height // (16 * n)))


def exchange(rows, orders):
    height, rank = rows.shape
    chunks, bits = len(orders), len(orders[0])
    size = height // chunks
    scratch = [pltpu.VMEM((chunks, size >> (k + 1), rank), jnp.bfloat16) for k in range(bits)]
    scratch += [pltpu.VMEM((chunks, size >> (k + 2), rank), jnp.bfloat16) for k in range(bits - 1)]
    scratch += [pltpu.VMEM((chunks, size >> (k + 2), rank), jnp.float32) for k in range(bits - 1)]
    scratch += [pltpu.SemaphoreType.DMA((2, bits, chunks))] * 2
    return pl.pallas_call(
        functools.partial(exchange_kernel, chunks, orders),
        out_shape=(
            jax.ShapeDtypeStruct(rows.shape, jnp.bfloat16),
            jax.ShapeDtypeStruct((rank, rank), jnp.float32),
        ),
        in_specs=[pl.BlockSpec(memory_space=pltpu.VMEM)],
        out_specs=(pl.BlockSpec(memory_space=pltpu.VMEM),) * 2,
        scratch_shapes=scratch,
        compiler_params=pltpu.CompilerParams(
            collective_id=0, has_side_effects=True, vmem_limit_bytes=40 * MIB
        ),
        name="exchange",
    )(rows)


def local(n, tile_values, tile_doc, tile_col, tile_count, panel):
    tile = tile_values.shape[1]
    rank = panel.shape[1]
    height = DOC_BLKS * tile
    hbm = pl.BlockSpec(memory_space=pltpu.HBM)
    vmem = pl.BlockSpec(memory_space=pltpu.VMEM)
    params = pltpu.CompilerParams(vmem_limit_bytes=40 * MIB)
    slots = [
        pltpu.SMEM(tile_count.shape, jnp.int32),
        pltpu.SMEM(tile_doc.shape, jnp.int32),
        pltpu.SMEM(tile_col.shape, jnp.int32),
        pltpu.VMEM(tile_values.shape, jnp.bfloat16),
    ]
    rows = pl.pallas_call(
        forward_kernel,
        out_shape=jax.ShapeDtypeStruct((height, rank), jnp.bfloat16),
        in_specs=[hbm] * 5,
        out_specs=vmem,
        scratch_shapes=slots
        + [
            pltpu.VMEM(panel.shape, jnp.bfloat16),
            pltpu.VMEM((height, rank), jnp.float32),
            pltpu.SemaphoreType.DMA((5,)),
        ],
        compiler_params=params,
        name="forward",
    )(tile_count, tile_doc, tile_col, tile_values, panel)
    rows, gram = exchange(rows, orders_of(n, height))
    return pl.pallas_call(
        backward_kernel,
        out_shape=jax.ShapeDtypeStruct(panel.shape, jnp.float32),
        in_specs=[hbm] * 4 + [vmem] * 2,
        out_specs=vmem,
        scratch_shapes=slots
        + [
            pltpu.VMEM((height, rank), jnp.bfloat16),
            pltpu.VMEM((rank, rank), jnp.float32),
            pltpu.VMEM((rank, rank), jnp.float32),
            pltpu.SemaphoreType.DMA((4,)),
        ],
        compiler_params=params,
        name="backward",
    )(tile_count, tile_doc, tile_col, tile_values, rows, gram)


def solution(mesh):
    return jax.shard_map(
        functools.partial(local, mesh.shape["term"]),
        mesh=mesh,
        in_specs=(
            P(("dom", "term"), None, None),
            P(("dom", "term")),
            P(("dom", "term")),
            P("dom"),
            P("term", None),
        ),
        out_specs=P(("dom", "term"), None),
        check_vma=False,
    )
```

```python
import functools

import jax
import jax.numpy as jnp
from jax import lax
from jax.experimental import pallas as pl
from jax.experimental.pallas import tpu as pltpu
from jax.sharding import PartitionSpec as P

DOC_BLKS = 32
GROUP = 8
MIB = 1024 * 1024

shift_ratio = 0.001


def each_slot(count, body):
    whole = count // GROUP

    def group(index, carry):
        body([index * GROUP + k for k in range(GROUP)])
        return carry

    def single(index, carry):
        body([index])
        return carry

    lax.fori_loop(0, whole, group, 0)
    lax.fori_loop(whole * GROUP, count, single, 0)


def start_copies(sources, targets, sems):
    copies = [
        pltpu.make_async_copy(source, target, sems.at[index])
        for index, (source, target) in enumerate(zip(sources, targets))
    ]
    for copy in copies:
        copy.start()
    return copies


def forward_kernel(
    count_hbm, doc_hbm, col_hbm, tiles_hbm, panel_hbm, rows_ref,
    count_ref, doc_ref, col_ref, tiles_ref, panel_ref, total, sems,
):
    tile = tiles_ref.shape[1]
    copies = start_copies(
        (count_hbm, doc_hbm, col_hbm, panel_hbm, tiles_hbm),
        (count_ref, doc_ref, col_ref, panel_ref, tiles_ref),
        sems,
    )
    total[...] = jnp.zeros_like(total)
    for copy in copies:
        copy.wait()
    count = count_ref[lax.axis_index("term")]

    def body(slots):
        products = []
        for slot in slots:
            start = pl.multiple_of(col_ref[slot] * tile, tile)
            products.append(
                jnp.dot(
                    tiles_ref[slot],
                    panel_ref[pl.ds(start, tile), :],
                    preferred_element_type=jnp.float32,
                )
            )
        for slot, product in zip(slots, products):
            start = pl.multiple_of(doc_ref[slot] * tile, tile)
            total[pl.ds(start, tile), :] += product

    each_slot(count, body)
    rows_ref[...] = total[...].astype(rows_ref.dtype)


def exchange_kernel(chunks, orders, x_ref, y_ref, gram_ref, *scratch):
    stages = len(orders[0])
    recv_bufs = scratch[:stages]
    send_bufs = scratch[stages : 2 * stages - 1]
    keep_bufs = scratch[2 * stages - 1 : 3 * stages - 2]
    send_sems, recv_sems = scratch[3 * stages - 2 :]
    me = lax.axis_index("term")
    rows = x_ref.shape[0] // chunks

    def width(bit):
        if isinstance(bit, tuple):
            return (1 << bit[0]) + ((1 << bit[1]) - (1 << bit[0])) * (me % 2)
        return 1 << bit

    def bit_of(bit):
        return (me // width(bit)) % 2

    def partner(bit):
        return me + width(bit) - 2 * width(bit) * bit_of(bit)

    barrier = pltpu.get_barrier_semaphore()
    bits = list(dict.fromkeys(bit for order in orders for bit in order))
    for bit in bits:
        pl.semaphore_signal(
            barrier, inc=1, device_id={"term": partner(bit)}, device_id_type=pl.DeviceIdType.MESH
        )
    pl.semaphore_wait(barrier, len(bits))

    started = []

    def send(phase, stage, chunk, bit, src, dst):
        copy = pltpu.make_async_remote_copy(
            src_ref=src,
            dst_ref=dst,
            send_sem=send_sems.at[phase, stage, chunk],
            recv_sem=recv_sems.at[phase, stage, chunk],
            device_id={"term": partner(bit)},
            device_id_type=pl.DeviceIdType.MESH,
        )
        copy.start()
        started.append(copy)
        return copy

    offsets = [[None] * (stages + 1) for _ in range(chunks)]
    reduce_copies = [[None] * stages for _ in range(chunks)]
    for chunk in range(chunks):
        offset = chunk * rows
        offsets[chunk][0] = offset
        for stage, bit in enumerate(orders[chunk]):
            half = rows >> (stage + 1)
            offset = offset + bit_of(bit) * half
            offsets[chunk][stage + 1] = offset
        half = rows // 2
        bit = orders[chunk][0]
        away = pl.multiple_of(chunk * rows + (1 - bit_of(bit)) * half, 16)
        reduce_copies[chunk][0] = send(
            0, 0, chunk, bit, x_ref.at[pl.ds(away, half)], recv_bufs[0].at[chunk]
        )

    def add_into(count, dst, dst_at, left, left_at, right, right_at):
        step = min(count, 64)

        def piece(index, carry):
            at = index * step

            def where(base):
                return pl.ds(pl.multiple_of(base + at, 16), step)

            value = left[where(left_at), :].astype(jnp.float32) + right[where(right_at), :].astype(
                jnp.float32
            )
            dst[where(dst_at), :] = value.astype(dst.dtype)
            return carry

        lax.fori_loop(0, count // step, piece, 0)

    gather_copies = [[None] * stages for _ in range(chunks)]

    def start_gather(chunk, stage):
        size = rows >> (stage + 1)
        at = pl.multiple_of(offsets[chunk][stage + 1], 16)
        block = y_ref.at[pl.ds(at, size)]
        gather_copies[chunk][stage] = send(1, stage, chunk, orders[chunk][stage], block, block)

    def reduce_step(stage, chunk):
        size = rows >> (stage + 1)
        reduce_copies[chunk][stage].wait_recv()
        got = recv_bufs[stage].at[chunk]
        if stage == 0:
            held, held_at = x_ref, offsets[chunk][1]
        else:
            held, held_at = keep_bufs[stage - 1].at[chunk], 0
        if stage == stages - 1:
            add_into(size, y_ref, offsets[chunk][stages], held, held_at, got, 0)
            start_gather(chunk, stage)
        else:
            bit = orders[chunk][stage + 1]
            half = size // 2
            mine, other = bit_of(bit) * half, (1 - bit_of(bit)) * half
            out = send_bufs[stage].at[chunk]
            add_into(half, out, 0, held, held_at + other, got, other)
            reduce_copies[chunk][stage + 1] = send(
                0, stage + 1, chunk, bit, out, recv_bufs[stage + 1].at[chunk]
            )
            add_into(half, keep_bufs[stage].at[chunk], 0, held, held_at + mine, got, mine)

    gram_ref[...] = jnp.zeros_like(gram_ref)

    def gather_step(stage, chunk):
        gather_copies[chunk][stage].wait_recv()
        if stage > 0:
            start_gather(chunk, stage - 1)
        else:
            block = y_ref[chunk * rows : (chunk + 1) * rows, :]
            gram_ref[...] += lax.dot_general(
                block, block, (((0,), (0,)), ((), ())), preferred_element_type=jnp.float32
            )

    for diagonal in range(2 * stages + chunks - 1):
        for chunk in range(chunks):
            step = diagonal - chunk
            if 0 <= step < stages:
                reduce_step(step, chunk)
            elif stages <= step < 2 * stages:
                gather_step(2 * stages - 1 - step, chunk)
    for copy in started:
        copy.wait_send()


def dot16(a, b, dims):
    return lax.dot_general(
        a.astype(jnp.bfloat16),
        b.astype(jnp.bfloat16),
        (dims, ((), ())),
        preferred_element_type=jnp.float32,
    )


def dot32(a, b, dims):
    return lax.dot_general(
        a, b, (dims, ((), ())), precision=lax.Precision.HIGHEST, preferred_element_type=jnp.float32
    )


def backward_kernel(
    count_hbm, doc_hbm, col_hbm, tiles_hbm, rows_ref, gram_ref, out_ref,
    count_ref, doc_ref, col_ref, tiles_ref, ortho, inverse, matrix, sems,
):
    tile = tiles_ref.shape[1]
    rank = rows_ref.shape[1]
    depth = 512
    copies = start_copies(
        (count_hbm, doc_hbm, col_hbm, tiles_hbm), (count_ref, doc_ref, col_ref, tiles_ref), sems
    )
    out_ref[...] = jnp.zeros_like(out_ref)
    row_ids = lax.broadcasted_iota(jnp.int32, (rank, rank), 0)
    lane_ids = lax.broadcasted_iota(jnp.int32, (rank, rank), 1)
    eye = (row_ids == lane_ids).astype(jnp.float32)
    gram = gram_ref[...]
    shift = shift_ratio * jnp.sum(gram * eye) / rank
    gram = gram + shift * eye
    scale_row = lax.rsqrt(jnp.sum(gram * eye, axis=0, keepdims=True))
    scale_col = lax.rsqrt(jnp.sum(gram * eye, axis=1, keepdims=True))
    gram = gram * scale_row * scale_col
    matrix[...] = gram
    inverse[...] = eye
    half_lower = jnp.where(row_ids > lane_ids, 1.0, jnp.where(row_ids == lane_ids, 0.5, 0.0))

    def newton(most, goal, dot):
        def unsolved(state):
            index, error = state
            return jnp.logical_and(index < most, jnp.logical_not(error < goal))

        def step(state):
            index, _ = state
            now = inverse[...]
            left = dot(now, matrix[...], ((1,), (0,)))
            gap = dot(left, now, ((1,), (1,))) - eye
            inverse[...] = now - dot(gap * half_lower, now, ((1,), (0,)))
            return index + 1, jnp.sum(gap * gap)

        _, error = lax.while_loop(unsolved, step, (0, jnp.float32(1e30)))
        return error

    newton(6, 0.1, dot16)
    error = newton(12, 1e-4, dot32)

    @pl.when(jnp.logical_not(error < 1e-4))
    def _():
        inverse[...] = eye
        lanes = lax.broadcasted_iota(jnp.int32, (1, rank), 1)

        def column(index, carry):
            pivot_row = matrix[pl.ds(index, 1), :]
            pivot = jnp.sum(jnp.where(lanes == index, pivot_row, 0.0), axis=1, keepdims=True)
            root = lax.rsqrt(pivot)
            factors = jnp.sum(
                jnp.where(lane_ids == index, matrix[...], 0.0), axis=1, keepdims=True
            )
            factors = jnp.where(row_ids[:, :1] > index, factors * root, 0.0)
            solved = inverse[pl.ds(index, 1), :] * root
            matrix[...] -= factors * (pivot_row * root)
            inverse[...] -= factors * solved
            inverse[pl.ds(index, 1), :] = solved
            return carry

        lax.fori_loop(0, rank, column, 0)

    whitener = (inverse[...] * scale_row).astype(jnp.bfloat16)

    def whiten_step(index, carry):
        where = pl.ds(pl.multiple_of(index * depth, depth), depth)
        ortho[where, :] = lax.dot_general(
            rows_ref[where, :],
            whitener,
            (((1,), (1,)), ((), ())),
            preferred_element_type=jnp.float32,
        ).astype(jnp.bfloat16)
        return carry

    lax.fori_loop(0, rows_ref.shape[0] // depth, whiten_step, 0)
    for copy in copies:
        copy.wait()
    count = count_ref[lax.axis_index("term")]

    def body(slots):
        products = []
        for slot in slots:
            start = pl.multiple_of(doc_ref[slot] * tile, tile)
            products.append(
                lax.dot_general(
                    tiles_ref[slot],
                    ortho[pl.ds(start, tile), :],
                    (((0,), (0,)), ((), ())),
                    preferred_element_type=jnp.float32,
                )
            )
        for slot, product in zip(slots, products):
            start = pl.multiple_of(col_ref[slot] * tile, tile)
            out_ref[pl.ds(start, tile), :] += product

    each_slot(count, body)


def orders_of(n, height):
    bits = n.bit_length() - 1
    order = [0, (2, 1), (1, 2)] + list(range(3, bits)) if bits > 2 else list(range(bits))
    return [order] * max(1, min(4, height // (16 * n)))


def exchange(rows, orders):
    height, rank = rows.shape
    chunks, bits = len(orders), len(orders[0])
    size = height // chunks
    scratch = [pltpu.VMEM((chunks, size >> (k + 1), rank), jnp.bfloat16) for k in range(bits)]
    scratch += [pltpu.VMEM((chunks, size >> (k + 2), rank), jnp.bfloat16) for k in range(bits - 1)]
    scratch += [pltpu.VMEM((chunks, size >> (k + 2), rank), jnp.float32) for k in range(bits - 1)]
    scratch += [pltpu.SemaphoreType.DMA((2, bits, chunks))] * 2
    return pl.pallas_call(
        functools.partial(exchange_kernel, chunks, orders),
        out_shape=(
            jax.ShapeDtypeStruct(rows.shape, jnp.bfloat16),
            jax.ShapeDtypeStruct((rank, rank), jnp.float32),
        ),
        in_specs=[pl.BlockSpec(memory_space=pltpu.VMEM)],
        out_specs=(pl.BlockSpec(memory_space=pltpu.VMEM),) * 2,
        scratch_shapes=scratch,
        compiler_params=pltpu.CompilerParams(
            collective_id=0, has_side_effects=True, vmem_limit_bytes=40 * MIB
        ),
        name="exchange",
    )(rows)


def local(n, tile_values, tile_doc, tile_col, tile_count, panel):
    tile = tile_values.shape[1]
    rank = panel.shape[1]
    height = DOC_BLKS * tile
    hbm = pl.BlockSpec(memory_space=pltpu.HBM)
    vmem = pl.BlockSpec(memory_space=pltpu.VMEM)
    params = pltpu.CompilerParams(vmem_limit_bytes=40 * MIB)
    slots = [
        pltpu.SMEM(tile_count.shape, jnp.int32),
        pltpu.SMEM(tile_doc.shape, jnp.int32),
        pltpu.SMEM(tile_col.shape, jnp.int32),
        pltpu.VMEM(tile_values.shape, jnp.bfloat16),
    ]
    rows = pl.pallas_call(
        forward_kernel,
        out_shape=jax.ShapeDtypeStruct((height, rank), jnp.bfloat16),
        in_specs=[hbm] * 5,
        out_specs=vmem,
        scratch_shapes=slots
        + [
            pltpu.VMEM(panel.shape, jnp.bfloat16),
            pltpu.VMEM((height, rank), jnp.float32),
            pltpu.SemaphoreType.DMA((5,)),
        ],
        compiler_params=pltpu.CompilerParams(vmem_limit_bytes=60 * MIB),
        name="forward",
    )(tile_count, tile_doc, tile_col, tile_values, panel)
    rows, gram = exchange(rows, orders_of(n, height))
    return pl.pallas_call(
        backward_kernel,
        out_shape=jax.ShapeDtypeStruct(panel.shape, jnp.float32),
        in_specs=[hbm] * 4 + [vmem] * 2,
        out_specs=vmem,
        scratch_shapes=slots
        + [
            pltpu.VMEM((height, rank), jnp.bfloat16),
            pltpu.VMEM((rank, rank), jnp.float32),
            pltpu.VMEM((rank, rank), jnp.float32),
            pltpu.SemaphoreType.DMA((4,)),
        ],
        compiler_params=params,
        name="backward",
    )(tile_count, tile_doc, tile_col, tile_values, rows, gram)


def solution(mesh):
    return jax.shard_map(
        functools.partial(local, mesh.shape["term"]),
        mesh=mesh,
        in_specs=(
            P(("dom", "term"), None, None),
            P(("dom", "term")),
            P(("dom", "term")),
            P("dom"),
            P("term", None),
        ),
        out_specs=P(("dom", "term"), None),
        check_vma=False,
    )
```

```python
import functools

import jax
import jax.numpy as jnp
from jax import lax
from jax.experimental import pallas as pl
from jax.experimental.pallas import tpu as pltpu
from jax.sharding import PartitionSpec as P

DOC_BLKS = 32
GROUP = 8
MIB = 1024 * 1024

shift_ratio = 0.001


def each_slot(count, body):
    whole = count // GROUP

    def group(index, carry):
        body([index * GROUP + k for k in range(GROUP)])
        return carry

    def single(index, carry):
        body([index])
        return carry

    lax.fori_loop(0, whole, group, 0)
    lax.fori_loop(whole * GROUP, count, single, 0)


def start_copies(sources, targets, sems):
    copies = [
        pltpu.make_async_copy(source, target, sems.at[index])
        for index, (source, target) in enumerate(zip(sources, targets))
    ]
    for copy in copies:
        copy.start()
    return copies


def forward_kernel(
    count_hbm, doc_hbm, col_hbm, tiles_hbm, panel_hbm, rows_ref,
    count_ref, doc_ref, col_ref, tiles_ref, panel_ref, total, sems,
):
    tile = tiles_ref.shape[1]
    copies = start_copies(
        (count_hbm, doc_hbm, col_hbm, panel_hbm, tiles_hbm),
        (count_ref, doc_ref, col_ref, panel_ref, tiles_ref),
        sems,
    )
    total[...] = jnp.zeros_like(total)
    for copy in copies:
        copy.wait()
    count = count_ref[lax.axis_index("term")]

    def body(slots):
        products = []
        for slot in slots:
            start = pl.multiple_of(col_ref[slot] * tile, tile)
            products.append(
                jnp.dot(
                    tiles_ref[slot],
                    panel_ref[pl.ds(start, tile), :],
                    preferred_element_type=jnp.float32,
                )
            )
        for slot, product in zip(slots, products):
            start = pl.multiple_of(doc_ref[slot] * tile, tile)
            total[pl.ds(start, tile), :] += product

    each_slot(count, body)
    rows_ref[...] = total[...].astype(rows_ref.dtype)


def exchange_kernel(chunks, orders, x_ref, y_ref, gram_ref, *scratch):
    stages = len(orders[0])
    recv_bufs = scratch[:stages]
    send_bufs = scratch[stages : 2 * stages - 1]
    keep_bufs = scratch[2 * stages - 1 : 3 * stages - 2]
    send_sems, recv_sems = scratch[3 * stages - 2 :]
    me = lax.axis_index("term")
    rows = x_ref.shape[0] // chunks

    def width(bit):
        if isinstance(bit, tuple):
            return (1 << bit[0]) + ((1 << bit[1]) - (1 << bit[0])) * (me % 2)
        return 1 << bit

    def bit_of(bit):
        return (me // width(bit)) % 2

    def partner(bit):
        return me + width(bit) - 2 * width(bit) * bit_of(bit)

    barrier = pltpu.get_barrier_semaphore()
    bits = list(dict.fromkeys(bit for order in orders for bit in order))
    for bit in bits:
        pl.semaphore_signal(
            barrier, inc=1, device_id={"term": partner(bit)}, device_id_type=pl.DeviceIdType.MESH
        )
    pl.semaphore_wait(barrier, len(bits))

    started = []

    def send(phase, stage, chunk, bit, src, dst):
        copy = pltpu.make_async_remote_copy(
            src_ref=src,
            dst_ref=dst,
            send_sem=send_sems.at[phase, stage, chunk],
            recv_sem=recv_sems.at[phase, stage, chunk],
            device_id={"term": partner(bit)},
            device_id_type=pl.DeviceIdType.MESH,
        )
        copy.start()
        started.append(copy)
        return copy

    offsets = [[None] * (stages + 1) for _ in range(chunks)]
    reduce_copies = [[None] * stages for _ in range(chunks)]
    for chunk in range(chunks):
        offset = chunk * rows
        offsets[chunk][0] = offset
        for stage, bit in enumerate(orders[chunk]):
            half = rows >> (stage + 1)
            offset = offset + bit_of(bit) * half
            offsets[chunk][stage + 1] = offset
        half = rows // 2
        bit = orders[chunk][0]
        away = pl.multiple_of(chunk * rows + (1 - bit_of(bit)) * half, 16)
        reduce_copies[chunk][0] = send(
            0, 0, chunk, bit, x_ref.at[pl.ds(away, half)], recv_bufs[0].at[chunk]
        )

    def add_into(count, dst, dst_at, left, left_at, right, right_at):
        step = min(count, 64)

        def piece(index, carry):
            at = index * step

            def where(base):
                return pl.ds(pl.multiple_of(base + at, 16), step)

            value = left[where(left_at), :].astype(jnp.float32) + right[where(right_at), :].astype(
                jnp.float32
            )
            dst[where(dst_at), :] = value.astype(dst.dtype)
            return carry

        lax.fori_loop(0, count // step, piece, 0)

    gather_copies = [[None] * stages for _ in range(chunks)]

    def start_gather(chunk, stage):
        size = rows >> (stage + 1)
        at = pl.multiple_of(offsets[chunk][stage + 1], 16)
        block = y_ref.at[pl.ds(at, size)]
        gather_copies[chunk][stage] = send(1, stage, chunk, orders[chunk][stage], block, block)

    def reduce_step(stage, chunk):
        size = rows >> (stage + 1)
        reduce_copies[chunk][stage].wait_recv()
        got = recv_bufs[stage].at[chunk]
        if stage == 0:
            held, held_at = x_ref, offsets[chunk][1]
        else:
            held, held_at = keep_bufs[stage - 1].at[chunk], 0
        if stage == stages - 1:
            add_into(size, y_ref, offsets[chunk][stages], held, held_at, got, 0)
            start_gather(chunk, stage)
        else:
            bit = orders[chunk][stage + 1]
            half = size // 2
            mine, other = bit_of(bit) * half, (1 - bit_of(bit)) * half
            out = send_bufs[stage].at[chunk]
            add_into(half, out, 0, held, held_at + other, got, other)
            reduce_copies[chunk][stage + 1] = send(
                0, stage + 1, chunk, bit, out, recv_bufs[stage + 1].at[chunk]
            )
            add_into(half, keep_bufs[stage].at[chunk], 0, held, held_at + mine, got, mine)

    gram_ref[...] = jnp.zeros_like(gram_ref)

    def gather_step(stage, chunk):
        gather_copies[chunk][stage].wait_recv()
        if stage > 0:
            start_gather(chunk, stage - 1)
        else:
            block = y_ref[chunk * rows : (chunk + 1) * rows, :]
            gram_ref[...] += lax.dot_general(
                block, block, (((0,), (0,)), ((), ())), preferred_element_type=jnp.float32
            )

    for diagonal in range(2 * stages + chunks - 1):
        for chunk in range(chunks):
            step = diagonal - chunk
            if 0 <= step < stages:
                reduce_step(step, chunk)
            elif stages <= step < 2 * stages:
                gather_step(2 * stages - 1 - step, chunk)
    for copy in started:
        copy.wait_send()


def dot16(a, b, dims):
    return lax.dot_general(
        a.astype(jnp.bfloat16),
        b.astype(jnp.bfloat16),
        (dims, ((), ())),
        preferred_element_type=jnp.float32,
    )


def dot32(a, b, dims):
    return lax.dot_general(
        a, b, (dims, ((), ())), precision=lax.Precision.HIGHEST, preferred_element_type=jnp.float32
    )


def backward_kernel(
    count_hbm, doc_hbm, col_hbm, tiles_hbm, rows_ref, gram_ref, out_ref,
    count_ref, doc_ref, col_ref, tiles_ref, ortho, inverse, matrix, sems,
):
    tile = tiles_ref.shape[1]
    rank = rows_ref.shape[1]
    depth = 512
    copies = start_copies(
        (count_hbm, doc_hbm, col_hbm, tiles_hbm), (count_ref, doc_ref, col_ref, tiles_ref), sems
    )
    out_ref[...] = jnp.zeros_like(out_ref)
    row_ids = lax.broadcasted_iota(jnp.int32, (rank, rank), 0)
    lane_ids = lax.broadcasted_iota(jnp.int32, (rank, rank), 1)
    eye = (row_ids == lane_ids).astype(jnp.float32)
    gram = gram_ref[...]
    shift = shift_ratio * jnp.sum(gram * eye) / rank
    gram = gram + shift * eye
    scale_row = lax.rsqrt(jnp.sum(gram * eye, axis=0, keepdims=True))
    scale_col = lax.rsqrt(jnp.sum(gram * eye, axis=1, keepdims=True))
    gram = gram * scale_row * scale_col
    matrix[...] = gram
    inverse[...] = eye
    half_lower = jnp.where(row_ids > lane_ids, 1.0, jnp.where(row_ids == lane_ids, 0.5, 0.0))

    def newton(most, goal, dot):
        def unsolved(state):
            index, error = state
            return jnp.logical_and(index < most, jnp.logical_not(error < goal))

        def step(state):
            index, _ = state
            now = inverse[...]
            left = dot(now, matrix[...], ((1,), (0,)))
            gap = dot(left, now, ((1,), (1,))) - eye
            inverse[...] = now - dot(gap * half_lower, now, ((1,), (0,)))
            return index + 1, jnp.sum(gap * gap)

        _, error = lax.while_loop(unsolved, step, (0, jnp.float32(1e30)))
        return error

    newton(6, 0.1, dot16)
    error = newton(12, 1e-4, dot32)

    turned = jnp.sum(jnp.where(inverse[...] * eye < 0.0, 1.0, 0.0))

    @pl.when(jnp.logical_not(jnp.logical_and(error < 1e-4, turned < 0.5)))
    def _():
        inverse[...] = eye
        lanes = lax.broadcasted_iota(jnp.int32, (1, rank), 1)

        def column(index, carry):
            pivot_row = matrix[pl.ds(index, 1), :]
            pivot = jnp.sum(jnp.where(lanes == index, pivot_row, 0.0), axis=1, keepdims=True)
            root = lax.rsqrt(pivot)
            factors = jnp.sum(
                jnp.where(lane_ids == index, matrix[...], 0.0), axis=1, keepdims=True
            )
            factors = jnp.where(row_ids[:, :1] > index, factors * root, 0.0)
            solved = inverse[pl.ds(index, 1), :] * root
            matrix[...] -= factors * (pivot_row * root)
            inverse[...] -= factors * solved
            inverse[pl.ds(index, 1), :] = solved
            return carry

        lax.fori_loop(0, rank, column, 0)

    whitener = (inverse[...] * scale_row).astype(jnp.bfloat16)

    def whiten_step(index, carry):
        where = pl.ds(pl.multiple_of(index * depth, depth), depth)
        ortho[where, :] = lax.dot_general(
            rows_ref[where, :],
            whitener,
            (((1,), (1,)), ((), ())),
            preferred_element_type=jnp.float32,
        ).astype(jnp.bfloat16)
        return carry

    lax.fori_loop(0, rows_ref.shape[0] // depth, whiten_step, 0)
    for copy in copies:
        copy.wait()
    count = count_ref[lax.axis_index("term")]

    def body(slots):
        products = []
        for slot in slots:
            start = pl.multiple_of(doc_ref[slot] * tile, tile)
            products.append(
                lax.dot_general(
                    tiles_ref[slot],
                    ortho[pl.ds(start, tile), :],
                    (((0,), (0,)), ((), ())),
                    preferred_element_type=jnp.float32,
                )
            )
        for slot, product in zip(slots, products):
            start = pl.multiple_of(col_ref[slot] * tile, tile)
            out_ref[pl.ds(start, tile), :] += product

    each_slot(count, body)


def orders_of(n, height):
    bits = n.bit_length() - 1
    order = [0, (2, 1), (1, 2)] + list(range(3, bits)) if bits > 2 else list(range(bits))
    return [order] * max(1, min(4, height // (16 * n)))


def exchange(rows, orders):
    height, rank = rows.shape
    chunks, bits = len(orders), len(orders[0])
    size = height // chunks
    scratch = [pltpu.VMEM((chunks, size >> (k + 1), rank), jnp.bfloat16) for k in range(bits)]
    scratch += [pltpu.VMEM((chunks, size >> (k + 2), rank), jnp.bfloat16) for k in range(bits - 1)]
    scratch += [pltpu.VMEM((chunks, size >> (k + 2), rank), jnp.float32) for k in range(bits - 1)]
    scratch += [pltpu.SemaphoreType.DMA((2, bits, chunks))] * 2
    return pl.pallas_call(
        functools.partial(exchange_kernel, chunks, orders),
        out_shape=(
            jax.ShapeDtypeStruct(rows.shape, jnp.bfloat16),
            jax.ShapeDtypeStruct((rank, rank), jnp.float32),
        ),
        in_specs=[pl.BlockSpec(memory_space=pltpu.VMEM)],
        out_specs=(pl.BlockSpec(memory_space=pltpu.VMEM),) * 2,
        scratch_shapes=scratch,
        compiler_params=pltpu.CompilerParams(
            collective_id=0, has_side_effects=True, vmem_limit_bytes=40 * MIB
        ),
        name="exchange",
    )(rows)


def local(n, tile_values, tile_doc, tile_col, tile_count, panel):
    tile = tile_values.shape[1]
    rank = panel.shape[1]
    height = DOC_BLKS * tile
    hbm = pl.BlockSpec(memory_space=pltpu.HBM)
    vmem = pl.BlockSpec(memory_space=pltpu.VMEM)
    params = pltpu.CompilerParams(vmem_limit_bytes=40 * MIB)
    slots = [
        pltpu.SMEM(tile_count.shape, jnp.int32),
        pltpu.SMEM(tile_doc.shape, jnp.int32),
        pltpu.SMEM(tile_col.shape, jnp.int32),
        pltpu.VMEM(tile_values.shape, jnp.bfloat16),
    ]
    rows = pl.pallas_call(
        forward_kernel,
        out_shape=jax.ShapeDtypeStruct((height, rank), jnp.bfloat16),
        in_specs=[hbm] * 5,
        out_specs=vmem,
        scratch_shapes=slots
        + [
            pltpu.VMEM(panel.shape, jnp.bfloat16),
            pltpu.VMEM((height, rank), jnp.float32),
            pltpu.SemaphoreType.DMA((5,)),
        ],
        compiler_params=pltpu.CompilerParams(vmem_limit_bytes=60 * MIB),
        name="forward",
    )(tile_count, tile_doc, tile_col, tile_values, panel)
    rows, gram = exchange(rows, orders_of(n, height))
    return pl.pallas_call(
        backward_kernel,
        out_shape=jax.ShapeDtypeStruct(panel.shape, jnp.float32),
        in_specs=[hbm] * 4 + [vmem] * 2,
        out_specs=vmem,
        scratch_shapes=slots
        + [
            pltpu.VMEM((height, rank), jnp.bfloat16),
            pltpu.VMEM((rank, rank), jnp.float32),
            pltpu.VMEM((rank, rank), jnp.float32),
            pltpu.SemaphoreType.DMA((4,)),
        ],
        compiler_params=params,
        name="backward",
    )(tile_count, tile_doc, tile_col, tile_values, rows, gram)


def solution(mesh):
    return jax.shard_map(
        functools.partial(local, mesh.shape["term"]),
        mesh=mesh,
        in_specs=(
            P(("dom", "term"), None, None),
            P(("dom", "term")),
            P(("dom", "term")),
            P("dom"),
            P("term", None),
        ),
        out_specs=P(("dom", "term"), None),
        check_vma=False,
    )
```

```python
import functools

import jax
import jax.numpy as jnp
from jax import lax
from jax.experimental import pallas as pl
from jax.experimental.pallas import tpu as pltpu
from jax.sharding import PartitionSpec as P

DOC_BLKS = 32
GROUP = 12
MIB = 1024 * 1024

shift_ratio = 0.001


def each_slot(count, body):
    whole = count // GROUP

    def group(index, carry):
        body([index * GROUP + k for k in range(GROUP)])
        return carry

    def single(index, carry):
        body([index])
        return carry

    lax.fori_loop(0, whole, group, 0)
    lax.fori_loop(whole * GROUP, count, single, 0)


def start_copies(sources, targets, sems):
    copies = [
        pltpu.make_async_copy(source, target, sems.at[index])
        for index, (source, target) in enumerate(zip(sources, targets))
    ]
    for copy in copies:
        copy.start()
    return copies


def forward_kernel(
    count_hbm, doc_hbm, col_hbm, tiles_hbm, panel_hbm, rows_ref,
    count_ref, doc_ref, col_ref, tiles_ref, panel_ref, total, sems,
):
    tile = tiles_ref.shape[1]
    copies = start_copies(
        (count_hbm, doc_hbm, col_hbm, panel_hbm, tiles_hbm),
        (count_ref, doc_ref, col_ref, panel_ref, tiles_ref),
        sems,
    )
    total[...] = jnp.zeros_like(total)
    for copy in copies:
        copy.wait()
    count = count_ref[lax.axis_index("term")]

    def body(slots):
        products = []
        for slot in slots:
            start = pl.multiple_of(col_ref[slot] * tile, tile)
            products.append(
                jnp.dot(
                    tiles_ref[slot],
                    panel_ref[pl.ds(start, tile), :],
                    preferred_element_type=jnp.float32,
                )
            )
        for slot, product in zip(slots, products):
            start = pl.multiple_of(doc_ref[slot] * tile, tile)
            total[pl.ds(start, tile), :] += product

    each_slot(count, body)
    rows_ref[...] = total[...].astype(rows_ref.dtype)


def exchange_kernel(chunks, orders, x_ref, y_ref, gram_ref, *scratch):
    stages = len(orders[0])
    recv_bufs = scratch[:stages]
    send_bufs = scratch[stages : 2 * stages - 1]
    keep_bufs = scratch[2 * stages - 1 : 3 * stages - 2]
    send_sems, recv_sems = scratch[3 * stages - 2 :]
    me = lax.axis_index("term")
    rows = x_ref.shape[0] // chunks

    def width(bit):
        if isinstance(bit, tuple):
            return (1 << bit[0]) + ((1 << bit[1]) - (1 << bit[0])) * (me % 2)
        return 1 << bit

    def bit_of(bit):
        return (me // width(bit)) % 2

    def partner(bit):
        return me + width(bit) - 2 * width(bit) * bit_of(bit)

    barrier = pltpu.get_barrier_semaphore()
    bits = list(dict.fromkeys(bit for order in orders for bit in order))
    for bit in bits:
        pl.semaphore_signal(
            barrier, inc=1, device_id={"term": partner(bit)}, device_id_type=pl.DeviceIdType.MESH
        )
    pl.semaphore_wait(barrier, len(bits))

    started = []

    def send(phase, stage, chunk, bit, src, dst):
        copy = pltpu.make_async_remote_copy(
            src_ref=src,
            dst_ref=dst,
            send_sem=send_sems.at[phase, stage, chunk],
            recv_sem=recv_sems.at[phase, stage, chunk],
            device_id={"term": partner(bit)},
            device_id_type=pl.DeviceIdType.MESH,
        )
        copy.start()
        started.append(copy)
        return copy

    offsets = [[None] * (stages + 1) for _ in range(chunks)]
    reduce_copies = [[None] * stages for _ in range(chunks)]
    for chunk in range(chunks):
        offset = chunk * rows
        offsets[chunk][0] = offset
        for stage, bit in enumerate(orders[chunk]):
            half = rows >> (stage + 1)
            offset = offset + bit_of(bit) * half
            offsets[chunk][stage + 1] = offset
        half = rows // 2
        bit = orders[chunk][0]
        away = pl.multiple_of(chunk * rows + (1 - bit_of(bit)) * half, 16)
        reduce_copies[chunk][0] = send(
            0, 0, chunk, bit, x_ref.at[pl.ds(away, half)], recv_bufs[0].at[chunk]
        )

    def add_into(count, dst, dst_at, left, left_at, right, right_at):
        step = min(count, 64)

        def piece(index, carry):
            at = index * step

            def where(base):
                return pl.ds(pl.multiple_of(base + at, 16), step)

            value = left[where(left_at), :].astype(jnp.float32) + right[where(right_at), :].astype(
                jnp.float32
            )
            dst[where(dst_at), :] = value.astype(dst.dtype)
            return carry

        lax.fori_loop(0, count // step, piece, 0)

    gather_copies = [[None] * stages for _ in range(chunks)]

    def start_gather(chunk, stage):
        size = rows >> (stage + 1)
        at = pl.multiple_of(offsets[chunk][stage + 1], 16)
        block = y_ref.at[pl.ds(at, size)]
        gather_copies[chunk][stage] = send(1, stage, chunk, orders[chunk][stage], block, block)

    def reduce_step(stage, chunk):
        size = rows >> (stage + 1)
        reduce_copies[chunk][stage].wait_recv()
        got = recv_bufs[stage].at[chunk]
        if stage == 0:
            held, held_at = x_ref, offsets[chunk][1]
        else:
            held, held_at = keep_bufs[stage - 1].at[chunk], 0
        if stage == stages - 1:
            add_into(size, y_ref, offsets[chunk][stages], held, held_at, got, 0)
            start_gather(chunk, stage)
        else:
            bit = orders[chunk][stage + 1]
            half = size // 2
            mine, other = bit_of(bit) * half, (1 - bit_of(bit)) * half
            out = send_bufs[stage].at[chunk]
            add_into(half, out, 0, held, held_at + other, got, other)
            reduce_copies[chunk][stage + 1] = send(
                0, stage + 1, chunk, bit, out, recv_bufs[stage + 1].at[chunk]
            )
            add_into(half, keep_bufs[stage].at[chunk], 0, held, held_at + mine, got, mine)

    gram_ref[...] = jnp.zeros_like(gram_ref)

    def gather_step(stage, chunk):
        gather_copies[chunk][stage].wait_recv()
        if stage > 0:
            start_gather(chunk, stage - 1)
        else:
            block = y_ref[chunk * rows : (chunk + 1) * rows, :]
            gram_ref[...] += lax.dot_general(
                block, block, (((0,), (0,)), ((), ())), preferred_element_type=jnp.float32
            )

    for diagonal in range(2 * stages + chunks - 1):
        for chunk in range(chunks):
            step = diagonal - chunk
            if 0 <= step < stages:
                reduce_step(step, chunk)
            elif stages <= step < 2 * stages:
                gather_step(2 * stages - 1 - step, chunk)
    for copy in started:
        copy.wait_send()


def dot16(a, b, dims):
    return lax.dot_general(
        a.astype(jnp.bfloat16),
        b.astype(jnp.bfloat16),
        (dims, ((), ())),
        preferred_element_type=jnp.float32,
    )


def dot32(a, b, dims):
    return lax.dot_general(
        a, b, (dims, ((), ())), precision=lax.Precision.HIGHEST, preferred_element_type=jnp.float32
    )


def backward_kernel(
    count_hbm, doc_hbm, col_hbm, tiles_hbm, rows_ref, gram_ref, out_ref,
    count_ref, doc_ref, col_ref, tiles_ref, ortho, inverse, matrix, sems,
):
    tile = tiles_ref.shape[1]
    rank = rows_ref.shape[1]
    depth = 512
    copies = start_copies(
        (count_hbm, doc_hbm, col_hbm, tiles_hbm), (count_ref, doc_ref, col_ref, tiles_ref), sems
    )
    out_ref[...] = jnp.zeros_like(out_ref)
    row_ids = lax.broadcasted_iota(jnp.int32, (rank, rank), 0)
    lane_ids = lax.broadcasted_iota(jnp.int32, (rank, rank), 1)
    eye = (row_ids == lane_ids).astype(jnp.float32)
    gram = gram_ref[...]
    shift = shift_ratio * jnp.sum(gram * eye) / rank
    gram = gram + shift * eye
    scale_row = lax.rsqrt(jnp.sum(gram * eye, axis=0, keepdims=True))
    scale_col = lax.rsqrt(jnp.sum(gram * eye, axis=1, keepdims=True))
    gram = gram * scale_row * scale_col
    matrix[...] = gram
    inverse[...] = eye
    half_lower = jnp.where(row_ids > lane_ids, 1.0, jnp.where(row_ids == lane_ids, 0.5, 0.0))

    def newton(most, goal, dot):
        def unsolved(state):
            index, error = state
            return jnp.logical_and(index < most, jnp.logical_not(error < goal))

        def step(state):
            index, _ = state
            now = inverse[...]
            left = dot(now, matrix[...], ((1,), (0,)))
            gap = dot(left, now, ((1,), (1,))) - eye
            inverse[...] = now - dot(gap * half_lower, now, ((1,), (0,)))
            return index + 1, jnp.sum(gap * gap)

        _, error = lax.while_loop(unsolved, step, (0, jnp.float32(1e30)))
        return error

    newton(6, 0.1, dot16)
    error = newton(12, 1e-4, dot32)

    turned = jnp.sum(jnp.where(inverse[...] * eye < 0.0, 1.0, 0.0))

    @pl.when(jnp.logical_not(jnp.logical_and(error < 1e-4, turned < 0.5)))
    def _():
        inverse[...] = eye
        lanes = lax.broadcasted_iota(jnp.int32, (1, rank), 1)

        def column(index, carry):
            pivot_row = matrix[pl.ds(index, 1), :]
            pivot = jnp.sum(jnp.where(lanes == index, pivot_row, 0.0), axis=1, keepdims=True)
            root = lax.rsqrt(pivot)
            factors = jnp.sum(
                jnp.where(lane_ids == index, matrix[...], 0.0), axis=1, keepdims=True
            )
            factors = jnp.where(row_ids[:, :1] > index, factors * root, 0.0)
            solved = inverse[pl.ds(index, 1), :] * root
            matrix[...] -= factors * (pivot_row * root)
            inverse[...] -= factors * solved
            inverse[pl.ds(index, 1), :] = solved
            return carry

        lax.fori_loop(0, rank, column, 0)

    whitener = (inverse[...] * scale_row).astype(jnp.bfloat16)

    def whiten_step(index, carry):
        where = pl.ds(pl.multiple_of(index * depth, depth), depth)
        ortho[where, :] = lax.dot_general(
            rows_ref[where, :],
            whitener,
            (((1,), (1,)), ((), ())),
            preferred_element_type=jnp.float32,
        ).astype(jnp.bfloat16)
        return carry

    lax.fori_loop(0, rows_ref.shape[0] // depth, whiten_step, 0)
    for copy in copies:
        copy.wait()
    count = count_ref[lax.axis_index("term")]

    def body(slots):
        products = []
        for slot in slots:
            start = pl.multiple_of(doc_ref[slot] * tile, tile)
            products.append(
                lax.dot_general(
                    tiles_ref[slot],
                    ortho[pl.ds(start, tile), :],
                    (((0,), (0,)), ((), ())),
                    preferred_element_type=jnp.float32,
                )
            )
        for slot, product in zip(slots, products):
            start = pl.multiple_of(col_ref[slot] * tile, tile)
            out_ref[pl.ds(start, tile), :] += product

    each_slot(count, body)


def orders_of(n, height):
    bits = n.bit_length() - 1
    order = [0, (2, 1), (1, 2)] + list(range(3, bits)) if bits > 2 else list(range(bits))
    return [order] * max(1, min(4, height // (16 * n)))


def exchange(rows, orders):
    height, rank = rows.shape
    chunks, bits = len(orders), len(orders[0])
    size = height // chunks
    scratch = [pltpu.VMEM((chunks, size >> (k + 1), rank), jnp.bfloat16) for k in range(bits)]
    scratch += [pltpu.VMEM((chunks, size >> (k + 2), rank), jnp.bfloat16) for k in range(bits - 1)]
    scratch += [pltpu.VMEM((chunks, size >> (k + 2), rank), jnp.float32) for k in range(bits - 1)]
    scratch += [pltpu.SemaphoreType.DMA((2, bits, chunks))] * 2
    return pl.pallas_call(
        functools.partial(exchange_kernel, chunks, orders),
        out_shape=(
            jax.ShapeDtypeStruct(rows.shape, jnp.bfloat16),
            jax.ShapeDtypeStruct((rank, rank), jnp.float32),
        ),
        in_specs=[pl.BlockSpec(memory_space=pltpu.VMEM)],
        out_specs=(pl.BlockSpec(memory_space=pltpu.VMEM),) * 2,
        scratch_shapes=scratch,
        compiler_params=pltpu.CompilerParams(
            collective_id=0, has_side_effects=True, vmem_limit_bytes=40 * MIB
        ),
        name="exchange",
    )(rows)


def local(n, tile_values, tile_doc, tile_col, tile_count, panel):
    tile = tile_values.shape[1]
    rank = panel.shape[1]
    height = DOC_BLKS * tile
    hbm = pl.BlockSpec(memory_space=pltpu.HBM)
    vmem = pl.BlockSpec(memory_space=pltpu.VMEM)
    params = pltpu.CompilerParams(vmem_limit_bytes=40 * MIB)
    slots = [
        pltpu.SMEM(tile_count.shape, jnp.int32),
        pltpu.SMEM(tile_doc.shape, jnp.int32),
        pltpu.SMEM(tile_col.shape, jnp.int32),
        pltpu.VMEM(tile_values.shape, jnp.bfloat16),
    ]
    rows = pl.pallas_call(
        forward_kernel,
        out_shape=jax.ShapeDtypeStruct((height, rank), jnp.bfloat16),
        in_specs=[hbm] * 5,
        out_specs=vmem,
        scratch_shapes=slots
        + [
            pltpu.VMEM(panel.shape, jnp.bfloat16),
            pltpu.VMEM((height, rank), jnp.float32),
            pltpu.SemaphoreType.DMA((5,)),
        ],
        compiler_params=pltpu.CompilerParams(vmem_limit_bytes=60 * MIB),
        name="forward",
    )(tile_count, tile_doc, tile_col, tile_values, panel)
    rows, gram = exchange(rows, orders_of(n, height))
    return pl.pallas_call(
        backward_kernel,
        out_shape=jax.ShapeDtypeStruct(panel.shape, jnp.float32),
        in_specs=[hbm] * 4 + [vmem] * 2,
        out_specs=vmem,
        scratch_shapes=slots
        + [
            pltpu.VMEM((height, rank), jnp.bfloat16),
            pltpu.VMEM((rank, rank), jnp.float32),
            pltpu.VMEM((rank, rank), jnp.float32),
            pltpu.SemaphoreType.DMA((4,)),
        ],
        compiler_params=params,
        name="backward",
    )(tile_count, tile_doc, tile_col, tile_values, rows, gram)


def solution(mesh):
    return jax.shard_map(
        functools.partial(local, mesh.shape["term"]),
        mesh=mesh,
        in_specs=(
            P(("dom", "term"), None, None),
            P(("dom", "term")),
            P(("dom", "term")),
            P("dom"),
            P("term", None),
        ),
        out_specs=P(("dom", "term"), None),
        check_vma=False,
    )
```
